256 devices in a mesh: grp: 16 (over y_lo, z), blk: 16 (over x, y_hi, core).
Axes of the slice: x: 4, y: 4 (y_hi: 2, y_lo: 2; y = y_hi * 2 + y_lo), z: 8, core: 2. Of those that a mesh axis runs over, the one named last changes fastest.
Arguments:
- encoded_anchor: bfloat16 [131072, 256], P(('grp', 'blk')), parts along dimension 0, may hold values from -1 to 1
- encoded_target: bfloat16 [131072, 256], P(('grp', 'blk')), parts along dimension 0, may hold values from -1 to 1
- matched_target: int32 [131072], P(('grp', 'blk')), parts along dimension 0, may hold values from 0 to 8191, as said below
- anchor_logzeta: float32 [131072], P(('grp', 'blk')), parts along dimension 0, may hold values from 0 to 20, as said below
- target_logzeta_saved: float32 [131072], P(('grp', 'blk')), parts along dimension 0, may hold values from 0 to 20, as said below
- heat_values: float32 [64], P('grp'), parts along dimension 0, may hold values from 0 to 1
- matchup_position: int32 [16], P('grp'), parts along dimension 0, may hold values from 0 to 3
Outputs:
- gradient_view_a: float32 [131072, 256], P(('grp', 'blk')), parts along dimension 0
- gradient_view_b: float32 [131072, 256], P(('grp', 'blk')), parts along dimension 0
The draws below stay inside these ranges and needn't reach their ends.
There are 16 independent parts, one for each index of `grp`. The reference program is written for one: setup_inputs(seed, part) draws one part's arguments, and reference() takes and returns one part's arrays. A program takes and returns all parts, laid end to end along the dimension named above; each array names one. Nothing has to cross between parts.
Inputs may be any that keep to these rules, and one draw needn't show every extreme that they name: `matched_target`: each view-B node is the partner of exactly one view-A node. anchor_logzeta[i] is the log of the sum over j of exp(scores[i, j]), computed from the same unit vectors and temperature. target_logzeta_saved[j] is the log of the sum over i of exp(scores[i, j]).
All inputs are finite; a program needn't handle non-finite values.
Results may differ from the reference program's by a relative error of at most 0.0041.
Values may be sent and summed in bfloat16 or wider, within the bound.
A program may use at most 64 MiB of HBM per device.

```python
import math
import jax
import jax.numpy as jnp
from jax import lax

D = 256
ROWS = 512
MATCHUP_TALLY = 4
TOKENS = 8192


centroid_count = 1024


def pair_partner(key):
    return jax.random.permutation(jax.random.fold_in(key, 41), TOKENS).astype(jnp.int32)


def view_choice(key):
    return jax.random.randint(jax.random.fold_in(key, 42), (1,), 0, MATCHUP_TALLY, dtype=jnp.int32)


def matchup_heat_values(key):
    logs = jax.random.uniform(jax.random.fold_in(key, 43), (MATCHUP_TALLY,), jnp.float32, minval=math.log(0.15), maxval=math.log(0.4))
    return jnp.exp(logs)


def embedding_pair(key, sharp, common_share, spread, noise_level):
    matched_target = pair_partner(key)
    centroids = jax.random.normal(jax.random.fold_in(key, 51), (centroid_count, D), jnp.float32) / math.sqrt(D)
    common = jax.random.normal(jax.random.fold_in(key, 52), (D,), jnp.float32) / math.sqrt(D)
    logits = jax.random.normal(jax.random.fold_in(key, 53), (TOKENS, centroid_count), jnp.float32)
    tilt = jax.random.normal(jax.random.fold_in(key, 54), (TOKENS, centroid_count), jnp.float32)
    noise = jax.random.normal(jax.random.fold_in(key, 55), (TOKENS, D), jnp.float32) / math.sqrt(D)
    fresh = jax.random.normal(jax.random.fold_in(key, 56), (TOKENS, D), jnp.float32) / math.sqrt(D)
    logs_a = jax.random.uniform(jax.random.fold_in(key, 57), (TOKENS, 1), jnp.float32, minval=-spread, maxval=spread)
    logs_b = jax.random.uniform(jax.random.fold_in(key, 58), (TOKENS, 1), jnp.float32, minval=-spread, maxval=spread)
    mix_share = math.sqrt(1.0 - common_share * common_share - noise_level * noise_level)

    def mixture(values):
        probability_share = jax.nn.softmax(sharp * values, axis=1)
        probability_share = probability_share / jnp.sqrt(jnp.sum(probability_share * probability_share, axis=1, keepdims=True))
        return jnp.dot(probability_share, centroids, precision=lax.Precision.HIGHEST)
    content_a = common_share * common[None, :] + mix_share * mixture(logits) + noise_level * noise
    content_pos = common_share * common[None, :] + mix_share * mixture(logits + 0.4 * tilt) + noise_level * (0.6 * noise + 0.8 * fresh)
    content_b = jnp.zeros((TOKENS, D), jnp.float32).at[matched_target].set(content_pos)
    values_a = jnp.clip(content_a * jnp.exp(logs_a) * 0.3, -0.25, 0.25)
    values_b = jnp.clip(content_b * jnp.exp(logs_b) * 0.3, -0.25, 0.25)
    return (values_a.astype(jnp.bfloat16), values_b.astype(jnp.bfloat16))


def sphere_anchors(embed):
    floats = embed.astype(jnp.float32)
    inverse = lax.rsqrt(jnp.sum(floats * floats, axis=1, keepdims=True) + 1e-06)
    return (floats * inverse).astype(jnp.bfloat16)


def anchor_smoothmax(former_factor, latter_factor, heat_scale):
    blocks = former_factor.reshape(TOKENS // ROWS, ROWS, D)

    def one_block(tile_extent):
        cosine_logits = lax.dot_general(tile_extent, latter_factor, (((1,), (1,)), ((), ())), preferred_element_type=jnp.float32) / heat_scale
        return jax.nn.logsumexp(cosine_logits, axis=1)
    return lax.map(one_block, blocks).reshape(TOKENS)


def saved_lse(key, pair):
    mapping_array = matchup_heat_values(key)
    chosen_matchup = view_choice(key)
    heat_scale = jnp.sum(jnp.where(jnp.arange(MATCHUP_TALLY, dtype=jnp.int32) == chosen_matchup[0], mapping_array, jnp.zeros_like(mapping_array)))
    scaled_anchor_vectors = sphere_anchors(pair[0])
    scaled_target_vectors = sphere_anchors(pair[1])
    return (anchor_smoothmax(scaled_anchor_vectors, scaled_target_vectors, heat_scale), anchor_smoothmax(scaled_target_vectors, scaled_anchor_vectors, heat_scale))


def draw_matched_target(key, part):
    derivative_output = pair_partner(key)
    key = jax.random.fold_in(key, 3)
    return derivative_output


def draw_matchup_position(key, part):
    derivative_output = view_choice(key)
    key = jax.random.fold_in(key, 4)
    return derivative_output


def draw_heat_values(key, part):
    derivative_output = matchup_heat_values(key)
    key = jax.random.fold_in(key, 5)
    return derivative_output


def draw_encoded_anchor(key, part):
    pair = embedding_pair(key, 8.0, 0.2, 0.3, 0.2)
    key = jax.random.fold_in(key, 11)
    return pair[0]


def draw_encoded_target(key, part):
    pair = embedding_pair(key, 8.0, 0.2, 0.3, 0.2)
    key = jax.random.fold_in(key, 12)
    return pair[1]


def draw_anchor_logzeta(key, part):
    pair = embedding_pair(key, 8.0, 0.2, 0.3, 0.2)
    derivative_output = saved_lse(key, pair)
    key = jax.random.fold_in(key, 21)
    return derivative_output[0]


def draw_target_logzeta_saved(key, part):
    pair = embedding_pair(key, 8.0, 0.2, 0.3, 0.2)
    derivative_output = saved_lse(key, pair)
    key = jax.random.fold_in(key, 22)
    return derivative_output[1]


def setup_inputs(seed: int = 0, part: int = 0) -> dict:
    arg_keys = jax.random.split(jax.random.key(seed), 8)
    part_splits = jax.random.split(jax.random.fold_in(arg_keys[7], part), 8)
    return {
        "encoded_anchor": draw_encoded_anchor(jax.random.fold_in(jax.random.fold_in(arg_keys[7], part), 71), part),
        "encoded_target": draw_encoded_target(jax.random.fold_in(jax.random.fold_in(arg_keys[7], part), 71), part),
        "matched_target": draw_matched_target(jax.random.fold_in(jax.random.fold_in(arg_keys[7], part), 71), part),
        "anchor_logzeta": draw_anchor_logzeta(jax.random.fold_in(jax.random.fold_in(arg_keys[7], part), 71), part),
        "target_logzeta_saved": draw_target_logzeta_saved(jax.random.fold_in(jax.random.fold_in(arg_keys[7], part), 71), part),
        "heat_values": draw_heat_values(jax.random.fold_in(jax.random.fold_in(arg_keys[7], part), 71), part),
        "matchup_position": draw_matchup_position(jax.random.fold_in(jax.random.fold_in(arg_keys[7], part), 71), part),
    }


def normalize(embed):
    floats = embed.astype(jnp.float32)
    inverse = lax.rsqrt(lax.optimization_barrier(jnp.sum(floats * floats, axis=1, keepdims=True)) + 1e-06)
    unit_float = floats * inverse
    return (inverse, unit_float.astype(jnp.bfloat16), unit_float)

def probability_linkage(sphere_anchors, sphere_targets, anchor_logzeta_local, target_logzeta, matched_entries, target_extent, heat_scale):
    cosine_logits = lax.dot_general(sphere_anchors, sphere_targets, (((1,), (1,)), ((), ())), preferred_element_type=jnp.float32) / heat_scale
    paired = (matched_entries[:, None] == target_extent[None, :]).astype(jnp.float32)
    probability_share = jnp.exp(cosine_logits - anchor_logzeta_local[:, None]) + jnp.exp(cosine_logits - target_logzeta[None, :]) - 2.0 * paired
    return probability_share.astype(jnp.bfloat16)

def finalize_gradient(dunit, inverse, unit_float):
    return inverse * (dunit - unit_float * lax.optimization_barrier(jnp.sum(unit_float * dunit, axis=1, keepdims=True)))

def reference(encoded_anchor, encoded_target, matched_target, anchor_logzeta, target_logzeta_saved, heat_values, matchup_position):
    heat_scale = jnp.sum(jnp.where(jnp.arange(heat_values.shape[0], dtype=jnp.int32) == matchup_position[0], heat_values, jnp.zeros_like(heat_values)))
    reciprocal_length_anchor, scaled_anchor_vectors, float_anchor_vectors = normalize(encoded_anchor)
    reciprocal_length_target, scaled_target_vectors, float_target_vectors = normalize(encoded_target)
    target_extent = jnp.arange(TOKENS, dtype=jnp.int32)

    def sweep(accumulated_amount, block_index):
        first_block = (block_index * ROWS).astype(jnp.int32)
        tile_sphere_vectors = lax.dynamic_slice_in_dim(scaled_anchor_vectors, first_block, ROWS, 0)
        tile_anchor_logzeta = lax.dynamic_slice_in_dim(anchor_logzeta, first_block, ROWS, 0)
        tile_matched_entries = lax.dynamic_slice_in_dim(matched_target, first_block, ROWS, 0)
        probability_share = probability_linkage(tile_sphere_vectors, scaled_target_vectors, tile_anchor_logzeta, target_logzeta_saved, tile_matched_entries, target_extent, heat_scale)
        sphere_derivative_entries = jnp.dot(probability_share, scaled_target_vectors, preferred_element_type=jnp.float32) / heat_scale
        accumulated_amount = accumulated_amount + lax.dot_general(probability_share, tile_sphere_vectors, (((0,), (0,)), ((), ())), preferred_element_type=jnp.float32)
        return (accumulated_amount, sphere_derivative_entries)
    accumulated_amount, blocks = lax.scan(sweep, jnp.zeros((TOKENS, D), jnp.float32), jnp.arange(TOKENS // ROWS, dtype=jnp.int32))
    sphere_derivative_anchor = blocks.reshape(TOKENS, D)
    sphere_derivative_target = accumulated_amount / heat_scale
    return (finalize_gradient(sphere_derivative_anchor, reciprocal_length_anchor, float_anchor_vectors), finalize_gradient(sphere_derivative_target, reciprocal_length_target, float_target_vectors))
```

```python
import functools
import math

import jax
import jax.numpy as jnp
from jax import lax
from jax.experimental import pallas as pl
from jax.experimental.pallas import tpu as pltpu
from jax.sharding import PartitionSpec as P

MESH = pl.DeviceIdType.MESH
BF, F32 = jnp.bfloat16, jnp.float32
NT = (((1,), (1,)), ((), ()))


def unit_rows(block):
    floats = block.astype(F32)
    inverse = lax.rsqrt(jnp.sum(floats * floats, axis=1, keepdims=True) + 1e-06)
    return inverse, floats * inverse


def exchange_kernel(
    a_hbm, b_hbm, match_hbm, la_hbm, lb_hbm, heat, which,
    da_own, da_left, da_right, db_own, db_core, db_far,
    a_raw, b_raw, match_raw, la_raw, lb_raw,
    ua, uat, ub, aux, eb, ea_col, match_col, da, db, da_out, opp_in, db_out, core_in,
    in_sem, ga_send, ga_recv, gb_send, gb_recv, ra_send, ra_recv, rb_send, rb_recv,
):
    rows = a_hbm.shape[0]
    half = rows // 2
    grp, blk = lax.axis_index("grp"), lax.axis_index("blk")
    x, y, core = blk // 4, (blk // 2) % 2, blk % 2

    def at(px, py, pc):
        return (grp, px * 4 + py * 2 + pc)

    left, right = at((x + 3) % 4, y, core), at((x + 1) % 4, y, core)
    other, far = at(x, y, 1 - core), at(x, 1 - y, core)

    barrier = pltpu.get_barrier_semaphore()
    for peer in (left, right, other, far):
        pl.semaphore_signal(barrier, inc=1, device_id=peer, device_id_type=MESH)

    loads = [
        pltpu.make_async_copy(src, dst, in_sem.at[k])
        for k, (src, dst) in enumerate(
            ((a_hbm, a_raw), (b_hbm, b_raw), (match_hbm, match_raw), (la_hbm, la_raw), (lb_hbm, lb_raw))
        )
    ]
    for load in loads:
        load.start()

    temperature = jnp.float32(0.0)
    for k in range(heat.shape[0]):
        temperature += jnp.where(which[0] == k, heat[k], 0.0)
    scale = math.log2(math.e) / jnp.broadcast_to(temperature, (1, 1))

    def send(src, dst, send_sem, recv_sem, peer):
        copy = pltpu.make_async_remote_copy(
            src_ref=src, dst_ref=dst, send_sem=send_sem, recv_sem=recv_sem, device_id=peer, device_id_type=MESH
        )
        copy.start()
        return copy

    for load in loads:
        load.wait()
    aux[0, 0:4, :] = jnp.exp(-la_raw[...])
    aux[0, 4:8, :] = match_raw[...].astype(F32)
    eb[0] = jnp.exp(-lb_raw[...])
    ua[0] = unit_rows(a_raw[...])[1].astype(BF)
    ub[0] = unit_rows(b_raw[...])[1].astype(BF)

    block_of = (blk, blk - core + 1 - core, blk + 2 - 4 * y, blk + 2 - 4 * y - core + 1 - core)

    def spread(group, part, source):
        columns = aux[source].T
        for k in range(4):
            if k // 2 in part:
                into = pl.ds(k * 128, 128)
                ea_col[group, into, :] = jnp.broadcast_to(columns[:, k : k + 1], (128, 128))
                match_col[group, into, :] = jnp.broadcast_to(columns[:, 4 + k : 5 + k], (128, 128))

    def scores(group, j):
        raw = lax.dot_general(ua[group], ub[j], NT, preferred_element_type=F32)
        chance = jnp.exp2(raw * scale)
        ids = (lax.broadcasted_iota(jnp.int32, (1, rows), 1) + block_of[j] * rows).astype(F32)
        reps = rows // 128
        weight = jnp.concatenate([ea_col[group]] * reps, axis=1) + eb[j]
        paired = jnp.concatenate([match_col[group]] * reps, axis=1) == ids
        value = chance * weight
        return jnp.where(paired, value - 2.0, value).astype(BF)

    def pair(group, j, first_of_group, first_of_j):
        coupling = scores(group, j)
        rows_term = jnp.dot(coupling, ub[j], preferred_element_type=F32)
        columns_term = jnp.dot(uat[group], coupling, preferred_element_type=F32)
        into = da_own if group == 0 else da.at[group - 1]
        if first_of_group:
            into[...] = rows_term
        else:
            into[...] += rows_term
        into = db_own if j == 0 else db.at[j - 1]
        if first_of_j:
            into[...] = columns_term
        else:
            into[...] += columns_term

    uat[0] = ua[0].T
    spread(0, (0, 1), 0)
    pair(0, 0, True, True)

    pl.semaphore_wait(barrier, 4)

    first, second = pl.ds(0, half), pl.ds(half, half)
    aux_right = send(aux.at[0], aux.at[1], ga_send.at[0], ga_recv.at[0], right)
    aux_left = send(aux.at[0], aux.at[2], ga_send.at[1], ga_recv.at[1], left)
    early_right = send(ua.at[0, first], ua.at[1, first], ga_send.at[2], ga_recv.at[2], right)
    early_left = send(ua.at[0, second], ua.at[1, second], ga_send.at[3], ga_recv.at[3], left)
    eb_other = send(eb.at[0], eb.at[1], gb_send.at[0], gb_recv.at[0], other)
    eb_far = send(eb.at[0], eb.at[2], gb_send.at[1], gb_recv.at[1], far)
    b_other = send(ub.at[0], ub.at[1], gb_send.at[2], gb_recv.at[2], other)
    b_far = send(ub.at[0], ub.at[2], gb_send.at[3], gb_recv.at[3], far)

    eb_other.wait_recv()
    b_other.wait_recv()
    pair(0, 1, False, True)

    aux_right.wait_recv()
    aux_left.wait_recv()
    aux_on = send(aux.at[1], aux.at[3], ga_send.at[4], ga_recv.at[4], right)
    early_right.wait_recv()
    opp_right = send(ua.at[1, first], ua.at[2, first], ga_send.at[5], ga_recv.at[5], right)
    early_left.wait_recv()
    opp_left = send(ua.at[1, second], ua.at[2, second], ga_send.at[6], ga_recv.at[6], left)
    late_left = send(ua.at[0, first], ua.at[3, second], ga_send.at[7], ga_recv.at[7], left)
    late_right = send(ua.at[0, second], ua.at[3, first], ga_send.at[8], ga_recv.at[8], right)

    uat[1] = ua[1].T
    spread(1, (0,), 1)
    spread(1, (1,), 2)
    pair(1, 0, True, False)
    pair(1, 1, False, False)

    eb_far.wait_recv()
    eb_on = send(eb.at[2], eb.at[3], gb_send.at[4], gb_recv.at[4], other)
    b_far.wait_recv()
    b_on = send(ub.at[2], ub.at[3], gb_send.at[5], gb_recv.at[5], other)

    aux_on.wait_recv()
    opp_right.wait_recv()
    opp_left.wait_recv()
    uat[2] = ua[2].T
    spread(2, (0, 1), 3)
    pair(2, 0, True, False)
    pair(2, 1, False, False)
    pair(2, 2, False, True)
    eb_on.wait_recv()
    b_on.wait_recv()
    pair(2, 3, False, True)

    da_out[1] = da[1].astype(BF)
    part_right = send(da_out.at[1, first], opp_in.at[first], ra_send.at[0], ra_recv.at[0], right)
    part_left = send(da_out.at[1, second], opp_in.at[second], ra_send.at[1], ra_recv.at[1], left)

    pair(1, 2, False, False)
    pair(1, 3, False, False)
    da_out[0] = da[0].astype(BF)
    sum_left = send(da_out.at[0, first], da_right.at[first], ra_send.at[2], ra_recv.at[2], left)
    sum_right = send(da_out.at[0, second], da_left.at[second], ra_send.at[3], ra_recv.at[3], right)

    pair(0, 2, False, False)
    pair(0, 3, False, False)

    late_left.wait_recv()
    late_right.wait_recv()
    uat[3] = ua[3].T
    columns_left, columns_right = aux[1].T, aux[2].T
    for k in range(4):
        columns = columns_left if k < 2 else columns_right
        kk = (k + 2) % 4
        into = pl.ds(k * 128, 128)
        ea_col[3, into, :] = jnp.broadcast_to(columns[:, kk : kk + 1], (128, 128))
        match_col[3, into, :] = jnp.broadcast_to(columns[:, 4 + kk : 5 + kk], (128, 128))
    pair(3, 3, True, False)
    db_out[2] = db[2].astype(BF)
    core_on = send(db_out.at[2], core_in, rb_send.at[0], rb_recv.at[0], other)
    pair(3, 2, False, False)
    core_on.wait_recv()
    db_out[1] = (db[1] + core_in[...].astype(F32)).astype(BF)
    sum_far = send(db_out.at[1], db_far, rb_send.at[1], rb_recv.at[1], far)
    pair(3, 1, False, False)
    db_out[0] = db[0].astype(BF)
    sum_other = send(db_out.at[0], db_core, rb_send.at[2], rb_recv.at[2], other)
    pair(3, 0, False, False)

    part_right.wait_recv()
    part_left.wait_recv()
    da_out[2, 0:half, :] = (da[2, 0:half, :] + opp_in[half:rows, :].astype(F32)).astype(BF)
    da_out[2, half:rows, :] = (da[2, half:rows, :] + opp_in[0:half, :].astype(F32)).astype(BF)
    last_left = send(da_out.at[2, first], da_right.at[second], ra_send.at[4], ra_recv.at[4], left)
    last_right = send(da_out.at[2, second], da_left.at[first], ra_send.at[5], ra_recv.at[5], right)

    sum_left.wait_recv()
    sum_right.wait_recv()
    sum_other.wait_recv()
    last_left.wait_recv()
    last_right.wait_recv()
    sum_far.wait_recv()
    for copy in (
        aux_right, aux_left, early_right, early_left, aux_on, opp_right, opp_left, late_left, late_right,
        eb_other, eb_far, b_other, b_far, eb_on, b_on,
        part_right, part_left, sum_left, sum_right, last_left, last_right, core_on, sum_far, sum_other,
    ):
        copy.wait_send()


def finish_kernel(a, b, heat, which, da_own, da_left, da_right, db_own, db_core, db_far, out_a, out_b):
    temperature = jnp.float32(0.0)
    for k in range(heat.shape[0]):
        temperature += jnp.where(which[0] == k, heat[k], 0.0)
    scale = 1.0 / jnp.broadcast_to(temperature, (1, 1))

    def tangent(block, total):
        inverse, unit = unit_rows(block)
        dunit = total * scale
        return inverse * (dunit - unit * jnp.sum(unit * dunit, axis=1, keepdims=True))

    total_a = da_own[...] + da_left[...].astype(F32) + da_right[...].astype(F32)
    out_a[...] = tangent(a[...], total_a)
    total_b = db_own[...] + db_core[...].astype(F32) + db_far[...].astype(F32)
    out_b[...] = tangent(b[...], total_b.T)


def on_device(encoded_anchor, encoded_target, matched_target, anchor_logzeta, target_logzeta_saved, heat_values, matchup_position):
    rows, width = encoded_anchor.shape
    half = rows // 2
    anywhere = pl.BlockSpec(memory_space=pl.ANY)
    smem = pl.BlockSpec(memory_space=pltpu.SMEM)
    vmem = pl.BlockSpec(memory_space=pltpu.VMEM)
    dma = pltpu.SemaphoreType.DMA
    pieces = pl.pallas_call(
        exchange_kernel,
        out_shape=(
            jax.ShapeDtypeStruct((rows, width), F32),
            jax.ShapeDtypeStruct((rows, width), BF),
            jax.ShapeDtypeStruct((rows, width), BF),
            jax.ShapeDtypeStruct((width, rows), F32),
            jax.ShapeDtypeStruct((width, rows), BF),
            jax.ShapeDtypeStruct((width, rows), BF),
        ),
        in_specs=[anywhere] * 5 + [smem] * 2,
        out_specs=[vmem] * 6,
        scratch_shapes=[
            pltpu.VMEM((rows, width), BF),
            pltpu.VMEM((rows, width), BF),
            pltpu.VMEM((4, 128), jnp.int32),
            pltpu.VMEM((4, 128), F32),
            pltpu.VMEM((1, rows), F32),
            pltpu.VMEM((4, rows, width), BF),
            pltpu.VMEM((4, width, rows), BF),
            pltpu.VMEM((4, rows, width), BF),
            pltpu.VMEM((4, 8, 128), F32),
            pltpu.VMEM((4, 1, rows), F32),
            pltpu.VMEM((4, rows, 128), F32),
            pltpu.VMEM((4, rows, 128), F32),
            pltpu.VMEM((3, rows, width), F32),
            pltpu.VMEM((3, width, rows), F32),
            pltpu.VMEM((3, rows, width), BF),
            pltpu.VMEM((rows, width), BF),
            pltpu.VMEM((3, width, rows), BF),
            pltpu.VMEM((width, rows), BF),
            dma((5,)),
            dma((9,)),
            dma((9,)),
            dma((6,)),
            dma((6,)),
            dma((6,)),
            dma((6,)),
            dma((3,)),
            dma((3,)),
        ],
        compiler_params=pltpu.CompilerParams(collective_id=7, has_side_effects=True, vmem_limit_bytes=44 << 20),
    )(
        encoded_anchor,
        encoded_target,
        matched_target.reshape(4, 128),
        anchor_logzeta.reshape(4, 128),
        target_logzeta_saved.reshape(1, rows),
        heat_values,
        matchup_position,
    )
    return pl.pallas_call(
        finish_kernel,
        out_shape=(jax.ShapeDtypeStruct((rows, width), F32), jax.ShapeDtypeStruct((rows, width), F32)),
        in_specs=[vmem] * 2 + [smem] * 2 + [vmem] * 6,
        out_specs=[vmem] * 2,
        compiler_params=pltpu.CompilerParams(vmem_limit_bytes=32 << 20),
    )(encoded_anchor, encoded_target, heat_values, matchup_position, *pieces)


def solution(mesh):
    both = ("grp", "blk")
    return jax.shard_map(
        on_device,
        mesh=mesh,
        in_specs=(P(both, None), P(both, None), P(both), P(both), P(both), P("grp"), P("grp")),
        out_specs=(P(both, None), P(both, None)),
        check_vma=False,
    )
```

```python
import functools
import math

import jax
import jax.numpy as jnp
from jax import lax
from jax.experimental import pallas as pl
from jax.experimental.pallas import tpu as pltpu
from jax.sharding import PartitionSpec as P

MESH = pl.DeviceIdType.MESH
BF, F32 = jnp.bfloat16, jnp.float32
NT = (((1,), (1,)), ((), ()))
TN = (((0,), (0,)), ((), ()))


def unit_rows(block):
    floats = block.astype(F32)
    inverse = lax.rsqrt(jnp.sum(floats * floats, axis=1, keepdims=True) + 1e-06)
    return inverse, floats * inverse


def exchange_kernel(
    a_hbm, b_hbm, match_hbm, la_hbm, lb_hbm, heat_hbm, which,
    scale_out, a_own, b_own, da_own, da_left, da_right, db_own, db_core, db_far,
    a_in, b_in, ua, ub, match, la, lb, eb, ids, ea_col, match_col, da, db, da_out, opp_in, db_out, db_other, core_in, heat,
    in_sem, send_sems, recv_sems,
):
    rows = a_hbm.shape[0]
    half, quarter = rows // 2, rows // 4
    first, second = pl.ds(0, half), pl.ds(half, half)
    grp, blk = lax.axis_index("grp"), lax.axis_index("blk")
    x, y, core = blk // 4, (blk // 2) % 2, blk % 2

    def at(px, py, pc):
        return px * 4 + py * 2 + pc

    left, right = at((x + 3) % 4, y, core), at((x + 1) % 4, y, core)
    other, far, far_other = at(x, y, 1 - core), at(x, 1 - y, core), at(x, 1 - y, 1 - core)

    barrier = pltpu.get_barrier_semaphore()
    for peer in (left, right, other, far):
        pl.semaphore_signal(barrier, inc=1, device_id=(grp, peer), device_id_type=MESH)

    loads = [
        pltpu.make_async_copy(src, dst, in_sem.at[k])
        for k, (src, dst) in enumerate(
            ((a_hbm, a_own), (b_hbm, b_own), (match_hbm, match.at[0]), (la_hbm, la.at[0]), (lb_hbm, lb.at[0]),
             (heat_hbm, heat))
        )
    ]
    for load in loads:
        load.start()

    copies = []

    def send(src, dst, peer):
        k = len(copies)
        copy = pltpu.make_async_remote_copy(
            src_ref=src, dst_ref=dst, send_sem=send_sems.at[k], recv_sem=recv_sems.at[k],
            device_id=(grp, peer), device_id_type=MESH,
        )
        copy.start()
        copies.append(copy)
        return copy

    def take_a(group, pieces):
        ua[group] = unit_rows(a_own[...] if group == 0 else a_in[group - 1])[1].astype(BF)
        columns = {}
        for source in sorted({source for source, _ in pieces}):
            columns[source] = (jnp.exp(-la[source]).T, match[source].astype(F32).T)
        for k, (source, quarter) in enumerate(pieces):
            into = pl.ds(k * 128, 128)
            weights, partners = columns[source]
            ea_col[group, into, :] = jnp.broadcast_to(weights[:, quarter : quarter + 1], (128, 128))
            match_col[group, into, :] = jnp.broadcast_to(partners[:, quarter : quarter + 1], (128, 128))

    def take_b(j):
        ub[j] = unit_rows(b_own[...] if j == 0 else b_in[j - 1])[1].astype(BF)
        along = lax.broadcasted_iota(jnp.int32, (1, rows), 1)
        if j < 2:
            eb[j] = jnp.exp(-lb[j])
            numbers = along + (blk, other)[j] * rows
        else:
            part = slice(0, half) if j == 2 else slice(half, rows)
            eb[j] = jnp.exp(-jnp.concatenate([lb[2][:, part], lb[3][:, part]], axis=1))
            begin = (j - 2) * half
            numbers = jnp.where(along < half, along + (far * rows + begin), along + (far_other * rows + begin - half))
        ids[j] = numbers.astype(F32)

    begun = set()

    def add(into, term, key):
        if key in begun:
            into[...] += term
        else:
            into[...] = term
        begun.add(key)

    def raw_scores(group, j):
        return lax.dot_general(ua[group], ub[j], NT, preferred_element_type=F32)

    def spend(raw, group, j):
        chance = jnp.exp2(raw * scale)
        reps = rows // 128
        weight = jnp.concatenate([ea_col[group]] * reps, axis=1) + eb[j]
        paired = jnp.concatenate([match_col[group]] * reps, axis=1) == ids[j]
        value = chance * weight
        coupling = jnp.where(paired, value - 2.0, value).astype(BF)
        rows_term = jnp.dot(coupling, ub[j], preferred_element_type=F32)
        add(da_own if group == 0 else da.at[group - 1], rows_term, ("a", group))
        columns_term = lax.dot_general(coupling, ua[group], TN, preferred_element_type=F32)
        add(db_own if j == 0 else db.at[j - 1], columns_term, ("b", j))

    def pairs(*todo):
        ahead = raw_scores(*todo[0])
        for k, (group, j) in enumerate(todo):
            raw = ahead
            if k + 1 < len(todo):
                ahead = raw_scores(*todo[k + 1])
            spend(raw, group, j)

    pl.semaphore_wait(barrier, 4)
    quarters = [pl.ds(k * quarter, quarter) for k in range(4)]
    early_right = [send(a_hbm.at[quarters[k]], a_in.at[0, quarters[k]], right) for k in (0, 1)]
    early_left = [send(a_hbm.at[quarters[k]], a_in.at[0, quarters[k]], left) for k in (2, 3)]
    b_other = send(b_hbm, b_in.at[0], other)
    far_a = send(b_hbm.at[first], b_in.at[1, first], far)
    small_left = [send(match_hbm, match.at[2], left), send(la_hbm, la.at[2], left)]
    small_right = [send(match_hbm, match.at[1], right), send(la_hbm, la.at[1], right)]
    lb_other = send(lb_hbm, lb.at[1], other)
    lb_far = send(lb_hbm, lb.at[2], far)
    late_left = send(a_hbm.at[first], a_in.at[2, second], left)
    late_right = send(a_hbm.at[second], a_in.at[2, first], right)

    for load in loads:
        load.wait()
    temperature = jnp.float32(0.0)
    for k in range(heat.shape[0]):
        temperature += jnp.where(which[0] == k, heat[k], 0.0)
    scale = math.log2(math.e) / jnp.broadcast_to(temperature, (1, 1))
    scale_out[...] = jnp.broadcast_to(1.0 / jnp.broadcast_to(temperature, (1, 1)), (8, 128))
    take_a(0, [(0, 0), (0, 1), (0, 2), (0, 3)])
    take_b(0)
    pairs((0, 0))

    opp = []
    for k in (0, 1):
        early_right[k].wait_recv()
        opp.append(send(a_in.at[0, quarters[k]], a_in.at[1, quarters[k]], right))
        early_left[k].wait_recv()
        opp.append(send(a_in.at[0, quarters[k + 2]], a_in.at[1, quarters[k + 2]], left))
    far_b = send(b_hbm.at[second], b_in.at[2, first], far)
    for copy in small_left + small_right:
        copy.wait_recv()
    small_on = [send(match.at[1], match.at[3], right), send(la.at[1], la.at[3], right)]
    lb_far.wait_recv()
    lb_on = send(lb.at[2], lb.at[3], other)
    b_other.wait_recv()
    lb_other.wait_recv()

    take_b(1)
    take_a(1, [(1, 0), (1, 1), (2, 2), (2, 3)])
    pairs((0, 1), (1, 0), (1, 1))

    far_a.wait_recv()
    far_a_on = send(b_in.at[1, first], b_in.at[1, second], other)
    lb_on.wait_recv()
    far_a_on.wait_recv()
    take_b(2)
    pairs((0, 2), (1, 2))

    far_b.wait_recv()
    far_b_on = send(b_in.at[2, first], b_in.at[2, second], other)
    for copy in small_on + opp:
        copy.wait_recv()
    take_a(2, [(3, 0), (3, 1), (3, 2), (3, 3)])
    pairs((2, 0), (2, 1))

    far_b_on.wait_recv()
    take_b(3)
    pairs((2, 2), (2, 3))
    da_out[1] = da[1].astype(BF)
    part_right = send(da_out.at[1, first], opp_in.at[first], right)
    part_left = send(da_out.at[1, second], opp_in.at[second], left)

    late_left.wait_recv()
    late_right.wait_recv()
    take_a(3, [(1, 2), (1, 3), (2, 0), (2, 1)])
    pairs((3, 2), (1, 3))
    db_out[0] = db[1, half:rows].astype(BF)
    core_a = send(db_out.at[0], core_in.at[0], other)
    da_out[0] = da[0].astype(BF)
    sum_left = send(da_out.at[0, first], da_right.at[first], left)
    sum_right = send(da_out.at[0, second], da_left.at[second], right)

    pairs((0, 3), (3, 3))
    db_out[1] = db[2, half:rows].astype(BF)
    core_b = send(db_out.at[1], core_in.at[1], other)
    core_a.wait_recv()
    db_out[2] = (db[1, 0:half] + core_in[0].astype(F32)).astype(BF)
    sum_far_a = send(db_out.at[2], db_far.at[first], far)

    pairs((3, 1), (3, 0))
    core_b.wait_recv()
    db_out[3] = (db[2, 0:half] + core_in[1].astype(F32)).astype(BF)
    sum_far_b = send(db_out.at[3], db_far.at[second], far)
    db_other[...] = db[0].astype(BF)
    sum_other = send(db_other, db_core, other)

    part_right.wait_recv()
    part_left.wait_recv()
    da_out[2, 0:half, :] = (da[2, 0:half, :] + opp_in[half:rows, :].astype(F32)).astype(BF)
    da_out[2, half:rows, :] = (da[2, half:rows, :] + opp_in[0:half, :].astype(F32)).astype(BF)
    last_left = send(da_out.at[2, first], da_right.at[second], left)
    last_right = send(da_out.at[2, second], da_left.at[first], right)

    for copy in (sum_left, sum_right, sum_other, sum_far_a, last_left, last_right, sum_far_b):
        copy.wait_recv()
    for copy in copies:
        copy.wait_send()


def finish_kernel(
    scale, a, b, da_own, da_left, da_right, db_own, db_core, db_far, out_a, out_b, result, sems
):
    rows = a.shape[0]
    half = rows // 2
    by_temperature = scale[0:1, 0:1]

    def tangent(block, total):
        inverse, unit = unit_rows(block)
        dunit = total * by_temperature
        return inverse * (dunit - unit * jnp.sum(unit * dunit, axis=1, keepdims=True))

    copies = []
    for which, (block, total, parts, out) in enumerate(
        ((b, db_own, (db_core, db_far), out_b), (a, da_own, (da_left, da_right), out_a))
    ):
        for k in range(2):
            part = pl.ds(k * half, half)
            summed = total[part] + parts[0][part].astype(F32) + parts[1][part].astype(F32)
            result[which, part] = tangent(block[part], summed)
            copies.append(pltpu.make_async_copy(result.at[which, part], out.at[part], sems.at[2 * which + k]))
            copies[-1].start()
    for copy in copies:
        copy.wait()


def on_device(encoded_anchor, encoded_target, matched_target, anchor_logzeta, target_logzeta_saved, heat_values, matchup_position):
    rows, width = encoded_anchor.shape
    anywhere = pl.BlockSpec(memory_space=pl.ANY)
    vmem = pl.BlockSpec(memory_space=pltpu.VMEM)
    dma = pltpu.SemaphoreType.DMA
    block = jax.ShapeDtypeStruct((rows, width), BF)
    pieces = pl.pallas_call(
        exchange_kernel,
        out_shape=(
            jax.ShapeDtypeStruct((8, 128), F32),
            block,
            block,
            jax.ShapeDtypeStruct((rows, width), F32),
            block,
            block,
            jax.ShapeDtypeStruct((rows, width), F32),
            block,
            block,
        ),
        in_specs=[anywhere] * 6 + [pl.BlockSpec(memory_space=pltpu.SMEM)],
        out_specs=[vmem] * 9,
        scratch_shapes=[
            pltpu.VMEM((3, rows, width), BF),
            pltpu.VMEM((3, rows, width), BF),
            pltpu.VMEM((4, rows, width), BF),
            pltpu.VMEM((4, rows, width), BF),
            pltpu.VMEM((4, 4, 128), jnp.int32),
            pltpu.VMEM((4, 4, 128), F32),
            pltpu.VMEM((4, 1, rows), F32),
            pltpu.VMEM((4, 1, rows), F32),
            pltpu.VMEM((4, 1, rows), F32),
            pltpu.VMEM((4, rows, 128), F32),
            pltpu.VMEM((4, rows, 128), F32),
            pltpu.VMEM((3, rows, width), F32),
            pltpu.VMEM((3, rows, width), F32),
            pltpu.VMEM((3, rows, width), BF),
            pltpu.VMEM((rows, width), BF),
            pltpu.VMEM((4, rows // 2, width), BF),
            pltpu.VMEM((rows, width), BF),
            pltpu.VMEM((2, rows // 2, width), BF),
            pltpu.SMEM((4,), F32),
            dma((6,)),
            dma((36,)),
            dma((36,)),
        ],
        compiler_params=pltpu.CompilerParams(collective_id=7, has_side_effects=True, vmem_limit_bytes=44 << 20),
    )(
        *(
            pltpu.with_memory_space_constraint(value, pltpu.HBM)
            for value in (
                encoded_anchor,
                encoded_target,
                matched_target.reshape(4, 128),
                anchor_logzeta.reshape(4, 128),
                target_logzeta_saved.reshape(1, rows),
                heat_values,
            )
        ),
        matchup_position,
    )
    return pl.pallas_call(
        finish_kernel,
        out_shape=(jax.ShapeDtypeStruct((rows, width), F32), jax.ShapeDtypeStruct((rows, width), F32)),
        in_specs=[vmem] * 9,
        out_specs=[anywhere] * 2,
        scratch_shapes=[pltpu.VMEM((2, rows, width), F32), dma((4,))],
        compiler_params=pltpu.CompilerParams(vmem_limit_bytes=32 << 20),
    )(*pieces)


def solution(mesh):
    both = ("grp", "blk")
    return jax.shard_map(
        on_device,
        mesh=mesh,
        in_specs=(P(both, None), P(both, None), P(both), P(both), P(both), P("grp"), P("grp")),
        out_specs=(P(both, None), P(both, None)),
        check_vma=False,
    )
```

```python
import functools
import math

import jax
import jax.numpy as jnp
from jax import lax
from jax.experimental import pallas as pl
from jax.experimental.pallas import tpu as pltpu
from jax.sharding import PartitionSpec as P

MESH = pl.DeviceIdType.MESH
BF, F32 = jnp.bfloat16, jnp.float32
NT = (((1,), (1,)), ((), ()))
TN = (((0,), (0,)), ((), ()))


def unit_rows(block):
    floats = block.astype(F32)
    inverse = lax.rsqrt(jnp.sum(floats * floats, axis=1, keepdims=True) + 1e-06)
    return inverse, floats * inverse


def exchange_kernel(
    a_hbm, b_hbm, match_hbm, la_hbm, lb_hbm, heat_hbm, which,
    scale_out, a_own, b_own, da_own, da_left, da_right, db_own, db_core, db_far,
    a_in, b_in, ua, ub, match, la, lb, eb, ids, ea_col, match_col, da, db, da_out, opp_in, db_out, db_other, core_in, heat,
    in_sem, send_sems, recv_sems,
):
    rows = a_hbm.shape[0]
    half, quarter = rows // 2, rows // 4
    first, second = pl.ds(0, half), pl.ds(half, half)
    grp, blk = lax.axis_index("grp"), lax.axis_index("blk")
    x, y, core = blk // 4, (blk // 2) % 2, blk % 2

    def at(px, py, pc):
        return px * 4 + py * 2 + pc

    left, right = at((x + 3) % 4, y, core), at((x + 1) % 4, y, core)
    other, far, far_other = at(x, y, 1 - core), at(x, 1 - y, core), at(x, 1 - y, 1 - core)

    barrier = pltpu.get_barrier_semaphore()
    for peer in (left, right, other, far):
        pl.semaphore_signal(barrier, inc=1, device_id=(grp, peer), device_id_type=MESH)

    loads = [
        pltpu.make_async_copy(src, dst, in_sem.at[k])
        for k, (src, dst) in enumerate(
            ((a_hbm, a_own), (b_hbm, b_own), (match_hbm, match.at[0]), (la_hbm, la.at[0]), (lb_hbm, lb.at[0]),
             (heat_hbm, heat))
        )
    ]
    for load in loads:
        load.start()

    copies = []

    def send(src, dst, peer):
        k = len(copies)
        copy = pltpu.make_async_remote_copy(
            src_ref=src, dst_ref=dst, send_sem=send_sems.at[k], recv_sem=recv_sems.at[k],
            device_id=(grp, peer), device_id_type=MESH,
        )
        copy.start()
        copies.append(copy)
        return copy

    def take_a(group, pieces):
        ua[group] = unit_rows(a_own[...] if group == 0 else a_in[group - 1])[1].astype(BF)
        columns = {}
        for source in sorted({source for source, _ in pieces}):
            columns[source] = (jnp.exp(-la[source]).T, match[source].astype(F32).T)
        for k, (source, quarter) in enumerate(pieces):
            into = pl.ds(k * 128, 128)
            weights, partners = columns[source]
            ea_col[group, into, :] = jnp.broadcast_to(weights[:, quarter : quarter + 1], (128, 128))
            match_col[group, into, :] = jnp.broadcast_to(partners[:, quarter : quarter + 1], (128, 128))

    def take_b(j, part):
        into = pl.ds(part * half, half)
        ub[j, into] = unit_rows((b_own if j == 0 else b_in.at[j - 1])[into])[1].astype(BF)
        if j < 2:
            source, owner, begin = j, (blk, other)[j], part * half
        else:
            source, owner, begin = 2 + part, (far, far_other)[part], (j - 2) * half
        eb[j, :, part * half : part * half + half] = jnp.exp(-lb[source, :, begin : begin + half])
        along = lax.broadcasted_iota(jnp.int32, (1, half), 1)
        ids[j, :, part * half : part * half + half] = (along + (owner * rows + begin)).astype(F32)

    begun = set()

    def add(into, term, key):
        if key in begun:
            into[...] += term
        else:
            into[...] = term
        begun.add(key)

    def raw_scores(group, j, part):
        return lax.dot_general(ua[group], ub[j, pl.ds(part * half, half)], NT, preferred_element_type=F32)

    def spend(raw, group, j, part):
        here = pl.ds(part * half, half)
        along = slice(part * half, part * half + half)
        chance = jnp.exp2(raw * scale)
        reps = half // 128
        weight = jnp.concatenate([ea_col[group]] * reps, axis=1) + eb[j, :, along]
        paired = jnp.concatenate([match_col[group]] * reps, axis=1) == ids[j, :, along]
        value = chance * weight
        coupling = jnp.where(paired, value - 2.0, value).astype(BF)
        rows_term = jnp.dot(coupling, ub[j, here], preferred_element_type=F32)
        add(da_own if group == 0 else da.at[group - 1], rows_term, ("a", group))
        columns_term = lax.dot_general(coupling, ua[group], TN, preferred_element_type=F32)
        add((db_own if j == 0 else db.at[j - 1]).at[here], columns_term, ("b", j, part))

    def pairs(*todo):
        units = []
        for group, j, *part in todo:
            units += [(group, j, p) for p in (part or (0, 1))]
        ahead = raw_scores(*units[0])
        for k, unit in enumerate(units):
            raw = ahead
            if k + 1 < len(units):
                ahead = raw_scores(*units[k + 1])
            spend(raw, *unit)

    pl.semaphore_wait(barrier, 4)
    quarters = [pl.ds(k * quarter, quarter) for k in range(4)]
    small_left = [send(match_hbm, match.at[2], left), send(la_hbm, la.at[2], left)]
    small_right = [send(match_hbm, match.at[1], right), send(la_hbm, la.at[1], right)]
    lb_other = send(lb_hbm, lb.at[1], other)
    lb_far = send(lb_hbm, lb.at[2], far)
    early_right = [send(a_hbm.at[quarters[k]], a_in.at[0, quarters[k]], right) for k in (0, 1)]
    early_left = [send(a_hbm.at[quarters[k]], a_in.at[0, quarters[k]], left) for k in (2, 3)]
    b_other = send(b_hbm, b_in.at[0], other)
    far_a = send(b_hbm.at[first], b_in.at[1, first], far)
    far_b = send(b_hbm.at[second], b_in.at[2, first], far)

    for load in loads:
        load.wait()
    temperature = jnp.float32(0.0)
    for k in range(heat.shape[0]):
        temperature += jnp.where(which[0] == k, heat[k], 0.0)
    scale = math.log2(math.e) / jnp.broadcast_to(temperature, (1, 1))
    scale_out[...] = jnp.broadcast_to(1.0 / jnp.broadcast_to(temperature, (1, 1)), (8, 128))
    take_a(0, [(0, 0), (0, 1), (0, 2), (0, 3)])
    take_b(0, 0)
    take_b(0, 1)
    pairs((0, 0))

    opp = []
    for k in (0, 1):
        early_right[k].wait_recv()
        opp.append(send(a_in.at[0, quarters[k]], a_in.at[1, quarters[k]], right))
        early_left[k].wait_recv()
        opp.append(send(a_in.at[0, quarters[k + 2]], a_in.at[1, quarters[k + 2]], left))
    for copy in small_left + small_right:
        copy.wait_recv()
    small_on = [send(match.at[1], match.at[3], right), send(la.at[1], la.at[3], right)]
    lb_far.wait_recv()
    lb_on = send(lb.at[2], lb.at[3], other)
    b_other.wait_recv()
    lb_other.wait_recv()

    take_b(1, 0)
    take_b(1, 1)
    take_a(1, [(1, 0), (1, 1), (2, 2), (2, 3)])
    pairs((0, 1), (1, 0))

    late_left = send(a_hbm.at[first], a_in.at[2, second], left)
    late_right = send(a_hbm.at[second], a_in.at[2, first], right)
    far_a.wait_recv()
    far_a_on = send(b_in.at[1, first], b_in.at[1, second], other)
    take_b(2, 0)
    pairs((1, 1), (1, 2, 0), (0, 2, 0))

    far_b.wait_recv()
    far_b_on = send(b_in.at[2, first], b_in.at[2, second], other)
    for copy in small_on + opp:
        copy.wait_recv()
    lb_on.wait_recv()
    far_a_on.wait_recv()
    take_a(2, [(3, 0), (3, 1), (3, 2), (3, 3)])
    take_b(2, 1)
    take_b(3, 0)
    pairs((2, 0), (2, 1), (2, 2), (2, 3, 0))

    far_b_on.wait_recv()
    take_b(3, 1)
    pairs((2, 3, 1))
    da_out[1] = da[1].astype(BF)
    part_right = send(da_out.at[1, first], opp_in.at[first], right)
    part_left = send(da_out.at[1, second], opp_in.at[second], left)
    pairs((1, 3, 0), (1, 3, 1), (1, 2, 1))
    da_out[0] = da[0].astype(BF)
    sum_left = send(da_out.at[0, first], da_right.at[first], left)
    sum_right = send(da_out.at[0, second], da_left.at[second], right)

    late_left.wait_recv()
    late_right.wait_recv()
    take_a(3, [(1, 2), (1, 3), (2, 0), (2, 1)])
    pairs((0, 2, 1), (3, 2, 1), (3, 2, 0))
    db_out[0] = db[1, half:rows].astype(BF)
    core_a = send(db_out.at[0], core_in.at[0], other)

    pairs((0, 3, 1), (3, 3, 1), (0, 3, 0), (3, 3, 0))
    db_out[1] = db[2, half:rows].astype(BF)
    core_b = send(db_out.at[1], core_in.at[1], other)
    core_a.wait_recv()
    db_out[2] = (db[1, 0:half] + core_in[0].astype(F32)).astype(BF)
    sum_far_a = send(db_out.at[2], db_far.at[first], far)

    pairs((3, 1), (3, 0))
    core_b.wait_recv()
    db_out[3] = (db[2, 0:half] + core_in[1].astype(F32)).astype(BF)
    sum_far_b = send(db_out.at[3], db_far.at[second], far)
    db_other[...] = db[0].astype(BF)
    sum_other = send(db_other, db_core, other)

    part_right.wait_recv()
    part_left.wait_recv()
    da_out[2, 0:half, :] = (da[2, 0:half, :] + opp_in[half:rows, :].astype(F32)).astype(BF)
    da_out[2, half:rows, :] = (da[2, half:rows, :] + opp_in[0:half, :].astype(F32)).astype(BF)
    last_left = send(da_out.at[2, first], da_right.at[second], left)
    last_right = send(da_out.at[2, second], da_left.at[first], right)

    for copy in (sum_left, sum_right, sum_other, sum_far_a, last_left, last_right, sum_far_b):
        copy.wait_recv()
    for copy in copies:
        copy.wait_send()


def finish_kernel(
    scale, a, b, da_own, da_left, da_right, db_own, db_core, db_far, out_a, out_b, result, sems
):
    rows = a.shape[0]
    half = rows // 2
    by_temperature = scale[0:1, 0:1]

    def tangent(block, total):
        inverse, unit = unit_rows(block)
        dunit = total * by_temperature
        return inverse * (dunit - unit * jnp.sum(unit * dunit, axis=1, keepdims=True))

    copies = []
    for which, (block, total, parts, out) in enumerate(
        ((b, db_own, (db_core, db_far), out_b), (a, da_own, (da_left, da_right), out_a))
    ):
        for k in range(2):
            part = pl.ds(k * half, half)
            summed = total[part] + parts[0][part].astype(F32) + parts[1][part].astype(F32)
            result[which, part] = tangent(block[part], summed)
            copies.append(pltpu.make_async_copy(result.at[which, part], out.at[part], sems.at[2 * which + k]))
            copies[-1].start()
    for copy in copies:
        copy.wait()


def on_device(encoded_anchor, encoded_target, matched_target, anchor_logzeta, target_logzeta_saved, heat_values, matchup_position):
    rows, width = encoded_anchor.shape
    anywhere = pl.BlockSpec(memory_space=pl.ANY)
    vmem = pl.BlockSpec(memory_space=pltpu.VMEM)
    dma = pltpu.SemaphoreType.DMA
    block = jax.ShapeDtypeStruct((rows, width), BF)
    pieces = pl.pallas_call(
        exchange_kernel,
        out_shape=(
            jax.ShapeDtypeStruct((8, 128), F32),
            block,
            block,
            jax.ShapeDtypeStruct((rows, width), F32),
            block,
            block,
            jax.ShapeDtypeStruct((rows, width), F32),
            block,
            block,
        ),
        in_specs=[anywhere] * 6 + [pl.BlockSpec(memory_space=pltpu.SMEM)],
        out_specs=[vmem] * 9,
        scratch_shapes=[
            pltpu.VMEM((3, rows, width), BF),
            pltpu.VMEM((3, rows, width), BF),
            pltpu.VMEM((4, rows, width), BF),
            pltpu.VMEM((4, rows, width), BF),
            pltpu.VMEM((4, 4, 128), jnp.int32),
            pltpu.VMEM((4, 4, 128), F32),
            pltpu.VMEM((4, 1, rows), F32),
            pltpu.VMEM((4, 1, rows), F32),
            pltpu.VMEM((4, 1, rows), F32),
            pltpu.VMEM((4, rows, 128), F32),
            pltpu.VMEM((4, rows, 128), F32),
            pltpu.VMEM((3, rows, width), F32),
            pltpu.VMEM((3, rows, width), F32),
            pltpu.VMEM((3, rows, width), BF),
            pltpu.VMEM((rows, width), BF),
            pltpu.VMEM((4, rows // 2, width), BF),
            pltpu.VMEM((rows, width), BF),
            pltpu.VMEM((2, rows // 2, width), BF),
            pltpu.SMEM((4,), F32),
            dma((6,)),
            dma((36,)),
            dma((36,)),
        ],
        compiler_params=pltpu.CompilerParams(collective_id=7, has_side_effects=True, vmem_limit_bytes=44 << 20),
    )(
        *(
            pltpu.with_memory_space_constraint(value, pltpu.HBM)
            for value in (
                encoded_anchor,
                encoded_target,
                matched_target.reshape(4, 128),
                anchor_logzeta.reshape(4, 128),
                target_logzeta_saved.reshape(1, rows),
                heat_values,
            )
        ),
        matchup_position,
    )
    return pl.pallas_call(
        finish_kernel,
        out_shape=(jax.ShapeDtypeStruct((rows, width), F32), jax.ShapeDtypeStruct((rows, width), F32)),
        in_specs=[vmem] * 9,
        out_specs=[anywhere] * 2,
        scratch_shapes=[pltpu.VMEM((2, rows, width), F32), dma((4,))],
        compiler_params=pltpu.CompilerParams(vmem_limit_bytes=32 << 20),
    )(*pieces)


def solution(mesh):
    both = ("grp", "blk")
    return jax.shard_map(
        on_device,
        mesh=mesh,
        in_specs=(P(both, None), P(both, None), P(both), P(both), P(both), P("grp"), P("grp")),
        out_specs=(P(both, None), P(both, None)),
        check_vma=False,
    )
```

```python
import functools
import math

import jax
import jax.numpy as jnp
from jax import lax
from jax.experimental import pallas as pl
from jax.experimental.pallas import tpu as pltpu
from jax.sharding import PartitionSpec as P

MESH = pl.DeviceIdType.MESH
BF, F32 = jnp.bfloat16, jnp.float32
NT = (((1,), (1,)), ((), ()))
TN = (((0,), (0,)), ((), ()))


def unit_rows(block):
    floats = block.astype(F32)
    inverse = lax.rsqrt(jnp.sum(floats * floats, axis=1, keepdims=True) + 1e-06)
    return inverse, floats * inverse


def exchange_kernel(
    a_hbm, b_hbm, match_hbm, la_hbm, lb_hbm, heat_hbm, which,
    scale_out, a_own, b_own, da_own, da_left, da_right, db_own, db_core, db_far,
    a_in, b_in, ua, ub, match, la, lb, eb, ids, ea_col, match_col, da, db, da_out, opp_in, db_out, db_other, core_in, heat,
    in_sem, send_sems, recv_sems,
):
    rows = a_hbm.shape[0]
    half, quarter = rows // 2, rows // 4
    first, second = pl.ds(0, half), pl.ds(half, half)
    grp, blk = lax.axis_index("grp"), lax.axis_index("blk")
    x, y, core = blk // 4, (blk // 2) % 2, blk % 2

    def at(px, py, pc):
        return px * 4 + py * 2 + pc

    left, right = at((x + 3) % 4, y, core), at((x + 1) % 4, y, core)
    other, far, far_other = at(x, y, 1 - core), at(x, 1 - y, core), at(x, 1 - y, 1 - core)

    barrier = pltpu.get_barrier_semaphore()
    for peer in (left, right, other, far):
        pl.semaphore_signal(barrier, inc=1, device_id=(grp, peer), device_id_type=MESH)

    loads = [
        pltpu.make_async_copy(src, dst, in_sem.at[k])
        for k, (src, dst) in enumerate(
            ((a_hbm, a_own), (b_hbm, b_own), (match_hbm, match.at[0]), (la_hbm, la.at[0]), (lb_hbm, lb.at[0]),
             (heat_hbm, heat))
        )
    ]
    for load in loads:
        load.start()

    copies = []

    def send(src, dst, peer):
        k = len(copies)
        copy = pltpu.make_async_remote_copy(
            src_ref=src, dst_ref=dst, send_sem=send_sems.at[k], recv_sem=recv_sems.at[k],
            device_id=(grp, peer), device_id_type=MESH,
        )
        copy.start()
        copies.append(copy)
        return copy

    def take_a(group, pieces):
        ua[group] = unit_rows(a_own[...] if group == 0 else a_in[group - 1])[1].astype(BF)
        columns = {}
        for source in sorted({source for source, _ in pieces}):
            columns[source] = (jnp.exp(-la[source]).T, match[source].astype(F32).T)
        for k, (source, quarter) in enumerate(pieces):
            into = pl.ds(k * 128, 128)
            weights, partners = columns[source]
            ea_col[group, into, :] = jnp.broadcast_to(weights[:, quarter : quarter + 1], (128, 128))
            match_col[group, into, :] = jnp.broadcast_to(partners[:, quarter : quarter + 1], (128, 128))

    def take_b(j, part):
        into = pl.ds(part * half, half)
        ub[j, into] = unit_rows((b_own if j == 0 else b_in.at[j - 1])[into])[1].astype(BF)
        if j < 2:
            source, owner, begin = j, (blk, other)[j], part * half
        else:
            source, owner, begin = 2 + part, (far, far_other)[part], (j - 2) * half
        eb[j, :, part * half : part * half + half] = jnp.exp(-lb[source, :, begin : begin + half])
        along = lax.broadcasted_iota(jnp.int32, (1, half), 1)
        ids[j, :, part * half : part * half + half] = (along + (owner * rows + begin)).astype(F32)

    begun = set()

    def add(into, term, key):
        if key in begun:
            into[...] += term
        else:
            into[...] = term
        begun.add(key)

    def raw_scores(group, j, part):
        return lax.dot_general(ua[group], ub[j, pl.ds(part * half, half)], NT, preferred_element_type=F32)

    def spend(raw, group, j, part):
        here = pl.ds(part * half, half)
        along = slice(part * half, part * half + half)
        chance = jnp.exp2(raw * scale)
        reps = half // 128
        weight = jnp.concatenate([ea_col[group]] * reps, axis=1) + eb[j, :, along]
        paired = jnp.concatenate([match_col[group]] * reps, axis=1) == ids[j, :, along]
        value = chance * weight
        coupling = jnp.where(paired, value - 2.0, value).astype(BF)
        rows_term = jnp.dot(coupling, ub[j, here], preferred_element_type=F32)
        add(da_own if group == 0 else da.at[group - 1], rows_term, ("a", group))
        columns_term = lax.dot_general(coupling, ua[group], TN, preferred_element_type=F32)
        add((db_own if j == 0 else db.at[j - 1]).at[here], columns_term, ("b", j, part))

    def pairs(*todo):
        units = []
        for group, j, *part in todo:
            units += [(group, j, p) for p in (part or (0, 1))]
        ahead = raw_scores(*units[0])
        for k, unit in enumerate(units):
            raw = ahead
            if k + 1 < len(units):
                ahead = raw_scores(*units[k + 1])
            spend(raw, *unit)

    pl.semaphore_wait(barrier, 4)
    quarters = [pl.ds(k * quarter, quarter) for k in range(4)]
    small_left = [send(match_hbm, match.at[2], left), send(la_hbm, la.at[2], left)]
    small_right = [send(match_hbm, match.at[1], right), send(la_hbm, la.at[1], right)]
    lb_other = send(lb_hbm, lb.at[1], other)
    lb_far = send(lb_hbm, lb.at[2], far)
    early_right = [send(a_hbm.at[quarters[k]], a_in.at[0, quarters[k]], right) for k in (0, 1)]
    early_left = [send(a_hbm.at[quarters[k]], a_in.at[0, quarters[k]], left) for k in (2, 3)]
    b_other = send(b_hbm, b_in.at[0], other)
    far_a = send(b_hbm.at[first], b_in.at[1, first], far)
    far_b = send(b_hbm.at[second], b_in.at[2, first], far)

    for load in loads:
        load.wait()
    temperature = jnp.float32(0.0)
    for k in range(heat.shape[0]):
        temperature += jnp.where(which[0] == k, heat[k], 0.0)
    scale = math.log2(math.e) / jnp.broadcast_to(temperature, (1, 1))
    scale_out[...] = jnp.broadcast_to(1.0 / jnp.broadcast_to(temperature, (1, 1)), (8, 128))
    take_a(0, [(0, 0), (0, 1), (0, 2), (0, 3)])
    take_b(0, 0)
    take_b(0, 1)
    pairs((0, 0))

    opp = []
    for k in (0, 1):
        early_right[k].wait_recv()
        opp.append(send(a_in.at[0, quarters[k]], a_in.at[1, quarters[k]], right))
        early_left[k].wait_recv()
        opp.append(send(a_in.at[0, quarters[k + 2]], a_in.at[1, quarters[k + 2]], left))
    for copy in small_left + small_right:
        copy.wait_recv()
    small_on = [send(match.at[1], match.at[3], right), send(la.at[1], la.at[3], right)]
    lb_far.wait_recv()
    lb_on = send(lb.at[2], lb.at[3], other)
    b_other.wait_recv()
    lb_other.wait_recv()

    take_b(1, 0)
    take_b(1, 1)
    take_a(1, [(1, 0), (1, 1), (2, 2), (2, 3)])
    pairs((0, 1), (1, 0))

    late_left = send(a_hbm.at[first], a_in.at[2, second], left)
    late_right = send(a_hbm.at[second], a_in.at[2, first], right)
    far_a.wait_recv()
    far_a_on = send(b_in.at[1, first], b_in.at[1, second], other)
    take_b(2, 0)
    pairs((1, 1), (1, 2, 0), (0, 2, 0))

    far_b.wait_recv()
    far_b_on = send(b_in.at[2, first], b_in.at[2, second], other)
    lb_on.wait_recv()
    far_a_on.wait_recv()
    take_b(2, 1)
    take_b(3, 0)
    pairs((1, 2, 1), (0, 2, 1))

    for copy in small_on + opp:
        copy.wait_recv()
    take_a(2, [(3, 0), (3, 1), (3, 2), (3, 3)])
    pairs((2, 0), (2, 1), (2, 2), (2, 3, 0))

    far_b_on.wait_recv()
    take_b(3, 1)
    pairs((2, 3, 1))
    da_out[1] = da[1].astype(BF)
    part_right = send(da_out.at[1, first], opp_in.at[first], right)
    part_left = send(da_out.at[1, second], opp_in.at[second], left)
    late_left.wait_recv()
    late_right.wait_recv()
    take_a(3, [(1, 2), (1, 3), (2, 0), (2, 1)])
    pairs((3, 2, 1), (3, 2, 0))
    db_out[0] = db[1, half:rows].astype(BF)
    core_a = send(db_out.at[0], core_in.at[0], other)

    pairs((1, 3), (0, 3))
    da_out[0] = da[0].astype(BF)
    sum_left = send(da_out.at[0, first], da_right.at[first], left)
    sum_right = send(da_out.at[0, second], da_left.at[second], right)
    core_a.wait_recv()
    db_out[2] = (db[1, 0:half] + core_in[0].astype(F32)).astype(BF)
    sum_far_a = send(db_out.at[2], db_far.at[first], far)

    pairs((3, 3, 1), (3, 3, 0))
    db_out[1] = db[2, half:rows].astype(BF)
    core_b = send(db_out.at[1], core_in.at[1], other)

    pairs((3, 1), (3, 0))
    core_b.wait_recv()
    db_out[3] = (db[2, 0:half] + core_in[1].astype(F32)).astype(BF)
    sum_far_b = send(db_out.at[3], db_far.at[second], far)
    db_other[...] = db[0].astype(BF)
    sum_other = send(db_other, db_core, other)

    part_right.wait_recv()
    part_left.wait_recv()
    da_out[2, 0:half, :] = (da[2, 0:half, :] + opp_in[half:rows, :].astype(F32)).astype(BF)
    da_out[2, half:rows, :] = (da[2, half:rows, :] + opp_in[0:half, :].astype(F32)).astype(BF)
    last_left = send(da_out.at[2, first], da_right.at[second], left)
    last_right = send(da_out.at[2, second], da_left.at[first], right)

    for copy in (sum_left, sum_right, sum_other, sum_far_a, last_left, last_right, sum_far_b):
        copy.wait_recv()
    for copy in copies:
        copy.wait_send()


def finish_kernel(
    scale, a, b, da_own, da_left, da_right, db_own, db_core, db_far, out_a, out_b, result, sems
):
    rows = a.shape[0]
    half = rows // 2
    by_temperature = scale[0:1, 0:1]

    def tangent(block, total):
        inverse, unit = unit_rows(block)
        dunit = total * by_temperature
        return inverse * (dunit - unit * jnp.sum(unit * dunit, axis=1, keepdims=True))

    copies = []
    for which, (block, total, parts, out) in enumerate(
        ((b, db_own, (db_core, db_far), out_b), (a, da_own, (da_left, da_right), out_a))
    ):
        for k in range(2):
            part = pl.ds(k * half, half)
            summed = total[part] + parts[0][part].astype(F32) + parts[1][part].astype(F32)
            result[which, part] = tangent(block[part], summed)
            copies.append(pltpu.make_async_copy(result.at[which, part], out.at[part], sems.at[2 * which + k]))
            copies[-1].start()
    for copy in copies:
        copy.wait()


def on_device(encoded_anchor, encoded_target, matched_target, anchor_logzeta, target_logzeta_saved, heat_values, matchup_position):
    rows, width = encoded_anchor.shape
    anywhere = pl.BlockSpec(memory_space=pl.ANY)
    vmem = pl.BlockSpec(memory_space=pltpu.VMEM)
    dma = pltpu.SemaphoreType.DMA
    block = jax.ShapeDtypeStruct((rows, width), BF)
    pieces = pl.pallas_call(
        exchange_kernel,
        out_shape=(
            jax.ShapeDtypeStruct((8, 128), F32),
            block,
            block,
            jax.ShapeDtypeStruct((rows, width), F32),
            block,
            block,
            jax.ShapeDtypeStruct((rows, width), F32),
            block,
            block,
        ),
        in_specs=[anywhere] * 6 + [pl.BlockSpec(memory_space=pltpu.SMEM)],
        out_specs=[vmem] * 9,
        scratch_shapes=[
            pltpu.VMEM((3, rows, width), BF),
            pltpu.VMEM((3, rows, width), BF),
            pltpu.VMEM((4, rows, width), BF),
            pltpu.VMEM((4, rows, width), BF),
            pltpu.VMEM((4, 4, 128), jnp.int32),
            pltpu.VMEM((4, 4, 128), F32),
            pltpu.VMEM((4, 1, rows), F32),
            pltpu.VMEM((4, 1, rows), F32),
            pltpu.VMEM((4, 1, rows), F32),
            pltpu.VMEM((4, rows, 128), F32),
            pltpu.VMEM((4, rows, 128), F32),
            pltpu.VMEM((3, rows, width), F32),
            pltpu.VMEM((3, rows, width), F32),
            pltpu.VMEM((3, rows, width), BF),
            pltpu.VMEM((rows, width), BF),
            pltpu.VMEM((4, rows // 2, width), BF),
            pltpu.VMEM((rows, width), BF),
            pltpu.VMEM((2, rows // 2, width), BF),
            pltpu.SMEM((4,), F32),
            dma((6,)),
            dma((36,)),
            dma((36,)),
        ],
        compiler_params=pltpu.CompilerParams(collective_id=7, has_side_effects=True, vmem_limit_bytes=44 << 20),
    )(
        *(
            pltpu.with_memory_space_constraint(value, pltpu.HBM)
            for value in (
                encoded_anchor,
                encoded_target,
                matched_target.reshape(4, 128),
                anchor_logzeta.reshape(4, 128),
                target_logzeta_saved.reshape(1, rows),
                heat_values,
            )
        ),
        matchup_position,
    )
    return pl.pallas_call(
        finish_kernel,
        out_shape=(jax.ShapeDtypeStruct((rows, width), F32), jax.ShapeDtypeStruct((rows, width), F32)),
        in_specs=[vmem] * 9,
        out_specs=[anywhere] * 2,
        scratch_shapes=[pltpu.VMEM((2, rows, width), F32), dma((4,))],
        compiler_params=pltpu.CompilerParams(vmem_limit_bytes=32 << 20),
    )(*pieces)


def solution(mesh):
    both = ("grp", "blk")
    return jax.shard_map(
        on_device,
        mesh=mesh,
        in_specs=(P(both, None), P(both, None), P(both), P(both), P(both), P("grp"), P("grp")),
        out_specs=(P(both, None), P(both, None)),
        check_vma=False,
    )
```

```python
import functools
import math

import jax
import jax.numpy as jnp
from jax import lax
from jax.experimental import pallas as pl
from jax.experimental.pallas import tpu as pltpu
from jax.sharding import PartitionSpec as P

MESH = pl.DeviceIdType.MESH
BF, F32 = jnp.bfloat16, jnp.float32
NT = (((1,), (1,)), ((), ()))
TN = (((0,), (0,)), ((), ()))


def unit_rows(block):
    floats = block.astype(F32)
    inverse = lax.rsqrt(jnp.sum(floats * floats, axis=1, keepdims=True) + 1e-06)
    return inverse, floats * inverse


def exchange_kernel(
    a_hbm, b_hbm, match_hbm, la_hbm, lb_hbm, heat_hbm, which,
    scale_out, a_own, b_own, da_own, da_left, da_right, db_own, db_core, db_far,
    a_in, b_in, ua, ub, match, la, lb, eb, ids, ea_col, match_col, da, db, da_out, opp_in, db_out, db_other, core_in, heat,
    in_sem, send_sems, recv_sems,
):
    rows = a_hbm.shape[0]
    half, quarter = rows // 2, rows // 4
    first, second = pl.ds(0, half), pl.ds(half, half)
    grp, blk = lax.axis_index("grp"), lax.axis_index("blk")
    x, y, core = blk // 4, (blk // 2) % 2, blk % 2

    def at(px, py, pc):
        return px * 4 + py * 2 + pc

    left, right = at((x + 3) % 4, y, core), at((x + 1) % 4, y, core)
    other, far, far_other = at(x, y, 1 - core), at(x, 1 - y, core), at(x, 1 - y, 1 - core)

    barrier = pltpu.get_barrier_semaphore()
    for peer in (left, right, other, far):
        pl.semaphore_signal(barrier, inc=1, device_id=(grp, peer), device_id_type=MESH)

    loads = [
        pltpu.make_async_copy(src, dst, in_sem.at[k])
        for k, (src, dst) in enumerate(
            ((a_hbm, a_own), (b_hbm, b_own), (match_hbm, match.at[0]), (la_hbm, la.at[0]), (lb_hbm, lb.at[0]),
             (heat_hbm, heat))
        )
    ]
    for load in loads:
        load.start()

    copies = []

    def send(src, dst, peer):
        k = len(copies)
        copy = pltpu.make_async_remote_copy(
            src_ref=src, dst_ref=dst, send_sem=send_sems.at[k], recv_sem=recv_sems.at[k],
            device_id=(grp, peer), device_id_type=MESH,
        )
        copy.start()
        copies.append(copy)
        return copy

    def take_a(group, pieces):
        ua[group] = unit_rows(a_own[...] if group == 0 else a_in[group - 1])[1].astype(BF)
        columns = {}
        for source in sorted({source for source, _ in pieces}):
            columns[source] = (jnp.exp(-la[source]).T, match[source].astype(F32).T)
        for k, (source, quarter) in enumerate(pieces):
            into = pl.ds(k * 128, 128)
            weights, partners = columns[source]
            ea_col[group, into, :] = jnp.broadcast_to(weights[:, quarter : quarter + 1], (128, 128))
            match_col[group, into, :] = jnp.broadcast_to(partners[:, quarter : quarter + 1], (128, 128))

    def take_b(j, part):
        into = pl.ds(part * half, half)
        ub[j, into] = unit_rows((b_own if j == 0 else b_in.at[j - 1])[into])[1].astype(BF)
        if j < 2:
            source, owner, begin = j, (blk, other)[j], part * half
        else:
            source, owner, begin = 2 + part, (far, far_other)[part], (j - 2) * half
        eb[j, :, part * half : part * half + half] = jnp.exp(-lb[source, :, begin : begin + half])
        along = lax.broadcasted_iota(jnp.int32, (1, half), 1)
        ids[j, :, part * half : part * half + half] = (along + (owner * rows + begin)).astype(F32)

    begun = set()

    def add(into, term, key):
        if key in begun:
            into[...] += term
        else:
            into[...] = term
        begun.add(key)

    def raw_scores(group, j, part):
        return lax.dot_general(ua[group], ub[j, pl.ds(part * half, half)], NT, preferred_element_type=F32)

    def spend(raw, group, j, part):
        here = pl.ds(part * half, half)
        along = slice(part * half, part * half + half)
        chance = jnp.exp2(raw * scale)
        reps = half // 128
        weight = jnp.concatenate([ea_col[group]] * reps, axis=1) + eb[j, :, along]
        paired = jnp.concatenate([match_col[group]] * reps, axis=1) == ids[j, :, along]
        value = chance * weight
        coupling = jnp.where(paired, value - 2.0, value).astype(BF)
        rows_term = jnp.dot(coupling, ub[j, here], preferred_element_type=F32)
        add(da_own if group == 0 else da.at[group - 1], rows_term, ("a", group))
        columns_term = lax.dot_general(coupling, ua[group], TN, preferred_element_type=F32)
        add((db_own if j == 0 else db.at[j - 1]).at[here], columns_term, ("b", j, part))

    def pairs(*todo):
        units = []
        for group, j, *part in todo:
            units += [(group, j, p) for p in (part or (0, 1))]
        ahead = raw_scores(*units[0])
        for k, unit in enumerate(units):
            raw = ahead
            if k + 1 < len(units):
                ahead = raw_scores(*units[k + 1])
            spend(raw, *unit)

    pl.semaphore_wait(barrier, 4)
    quarters = [pl.ds(k * quarter, quarter) for k in range(4)]
    small_left = [send(match_hbm, match.at[2], left), send(la_hbm, la.at[2], left)]
    small_right = [send(match_hbm, match.at[1], right), send(la_hbm, la.at[1], right)]
    lb_other = send(lb_hbm, lb.at[1], other)
    lb_far = send(lb_hbm, lb.at[2], far)
    early_right = [send(a_hbm.at[quarters[k]], a_in.at[0, quarters[k]], right) for k in (0, 1)]
    early_left = [send(a_hbm.at[quarters[k]], a_in.at[0, quarters[k]], left) for k in (2, 3)]
    b_other = send(b_hbm, b_in.at[0], other)
    far_a = send(b_hbm.at[first], b_in.at[1, first], far)
    far_b = send(b_hbm.at[second], b_in.at[2, first], far)

    for load in loads:
        load.wait()
    temperature = jnp.float32(0.0)
    for k in range(heat.shape[0]):
        temperature += jnp.where(which[0] == k, heat[k], 0.0)
    scale = math.log2(math.e) / jnp.broadcast_to(temperature, (1, 1))
    scale_out[...] = jnp.broadcast_to(1.0 / jnp.broadcast_to(temperature, (1, 1)), (8, 128))
    take_a(0, [(0, 0), (0, 1), (0, 2), (0, 3)])
    take_b(0, 0)
    take_b(0, 1)
    pairs((0, 0))
    b_other.wait_recv()
    lb_other.wait_recv()
    take_b(1, 0)
    take_b(1, 1)
    pairs((0, 1))

    opp = []
    for k in (0, 1):
        early_right[k].wait_recv()
        opp.append(send(a_in.at[0, quarters[k]], a_in.at[1, quarters[k]], right))
        early_left[k].wait_recv()
        opp.append(send(a_in.at[0, quarters[k + 2]], a_in.at[1, quarters[k + 2]], left))
    for copy in small_left + small_right:
        copy.wait_recv()
    small_on = [send(match.at[1], match.at[3], right), send(la.at[1], la.at[3], right)]
    lb_far.wait_recv()
    lb_on = send(lb.at[2], lb.at[3], other)

    take_a(1, [(1, 0), (1, 1), (2, 2), (2, 3)])
    pairs((1, 0), (1, 1))

    late_left = send(a_hbm.at[first], a_in.at[2, second], left)
    late_right = send(a_hbm.at[second], a_in.at[2, first], right)
    far_a.wait_recv()
    far_a_on = send(b_in.at[1, first], b_in.at[1, second], other)
    take_b(2, 0)
    pairs((1, 2, 0), (0, 2, 0))

    far_b.wait_recv()
    far_b_on = send(b_in.at[2, first], b_in.at[2, second], other)
    lb_on.wait_recv()
    far_a_on.wait_recv()
    take_b(2, 1)
    take_b(3, 0)
    pairs((1, 2, 1), (0, 2, 1))

    for copy in small_on + opp:
        copy.wait_recv()
    take_a(2, [(3, 0), (3, 1), (3, 2), (3, 3)])
    pairs((2, 0), (2, 1), (2, 2), (2, 3, 0))

    far_b_on.wait_recv()
    take_b(3, 1)
    pairs((2, 3, 1))
    da_out[1] = da[1].astype(BF)
    part_right = send(da_out.at[1, first], opp_in.at[first], right)
    part_left = send(da_out.at[1, second], opp_in.at[second], left)
    late_left.wait_recv()
    late_right.wait_recv()
    take_a(3, [(1, 2), (1, 3), (2, 0), (2, 1)])
    pairs((3, 2, 1), (3, 2, 0))
    db_out[0] = db[1, half:rows].astype(BF)
    core_a = send(db_out.at[0], core_in.at[0], other)

    pairs((1, 3), (0, 3))
    da_out[0] = da[0].astype(BF)
    sum_left = send(da_out.at[0, first], da_right.at[first], left)
    sum_right = send(da_out.at[0, second], da_left.at[second], right)
    core_a.wait_recv()
    db_out[2] = (db[1, 0:half] + core_in[0].astype(F32)).astype(BF)
    sum_far_a = send(db_out.at[2], db_far.at[first], far)

    pairs((3, 3, 1), (3, 3, 0))
    db_out[1] = db[2, half:rows].astype(BF)
    core_b = send(db_out.at[1], core_in.at[1], other)

    pairs((3, 1), (3, 0))
    core_b.wait_recv()
    db_out[3] = (db[2, 0:half] + core_in[1].astype(F32)).astype(BF)
    sum_far_b = send(db_out.at[3], db_far.at[second], far)
    db_other[...] = db[0].astype(BF)
    sum_other = send(db_other, db_core, other)

    part_right.wait_recv()
    part_left.wait_recv()
    da_out[2, 0:half, :] = (da[2, 0:half, :] + opp_in[half:rows, :].astype(F32)).astype(BF)
    da_out[2, half:rows, :] = (da[2, half:rows, :] + opp_in[0:half, :].astype(F32)).astype(BF)
    last_left = send(da_out.at[2, first], da_right.at[second], left)
    last_right = send(da_out.at[2, second], da_left.at[first], right)

    for copy in (sum_left, sum_right, sum_other, sum_far_a, last_left, last_right, sum_far_b):
        copy.wait_recv()
    for copy in copies:
        copy.wait_send()


def finish_kernel(
    scale, a, b, da_own, da_left, da_right, db_own, db_core, db_far, out_a, out_b, result, sems
):
    rows = a.shape[0]
    half = rows // 2
    by_temperature = scale[0:1, 0:1]

    def tangent(block, total):
        inverse, unit = unit_rows(block)
        dunit = total * by_temperature
        return inverse * (dunit - unit * jnp.sum(unit * dunit, axis=1, keepdims=True))

    copies = []
    for which, (block, total, parts, out) in enumerate(
        ((b, db_own, (db_core, db_far), out_b), (a, da_own, (da_left, da_right), out_a))
    ):
        for k in range(2):
            part = pl.ds(k * half, half)
            summed = total[part] + parts[0][part].astype(F32) + parts[1][part].astype(F32)
            result[which, part] = tangent(block[part], summed)
            copies.append(pltpu.make_async_copy(result.at[which, part], out.at[part], sems.at[2 * which + k]))
            copies[-1].start()
    for copy in copies:
        copy.wait()


def on_device(encoded_anchor, encoded_target, matched_target, anchor_logzeta, target_logzeta_saved, heat_values, matchup_position):
    rows, width = encoded_anchor.shape
    anywhere = pl.BlockSpec(memory_space=pl.ANY)
    vmem = pl.BlockSpec(memory_space=pltpu.VMEM)
    dma = pltpu.SemaphoreType.DMA
    block = jax.ShapeDtypeStruct((rows, width), BF)
    pieces = pl.pallas_call(
        exchange_kernel,
        out_shape=(
            jax.ShapeDtypeStruct((8, 128), F32),
            block,
            block,
            jax.ShapeDtypeStruct((rows, width), F32),
            block,
            block,
            jax.ShapeDtypeStruct((rows, width), F32),
            block,
            block,
        ),
        in_specs=[anywhere] * 6 + [pl.BlockSpec(memory_space=pltpu.SMEM)],
        out_specs=[vmem] * 9,
        scratch_shapes=[
            pltpu.VMEM((3, rows, width), BF),
            pltpu.VMEM((3, rows, width), BF),
            pltpu.VMEM((4, rows, width), BF),
            pltpu.VMEM((4, rows, width), BF),
            pltpu.VMEM((4, 4, 128), jnp.int32),
            pltpu.VMEM((4, 4, 128), F32),
            pltpu.VMEM((4, 1, rows), F32),
            pltpu.VMEM((4, 1, rows), F32),
            pltpu.VMEM((4, 1, rows), F32),
            pltpu.VMEM((4, rows, 128), F32),
            pltpu.VMEM((4, rows, 128), F32),
            pltpu.VMEM((3, rows, width), F32),
            pltpu.VMEM((3, rows, width), F32),
            pltpu.VMEM((3, rows, width), BF),
            pltpu.VMEM((rows, width), BF),
            pltpu.VMEM((4, rows // 2, width), BF),
            pltpu.VMEM((rows, width), BF),
            pltpu.VMEM((2, rows // 2, width), BF),
            pltpu.SMEM((4,), F32),
            dma((6,)),
            dma((36,)),
            dma((36,)),
        ],
        compiler_params=pltpu.CompilerParams(collective_id=7, has_side_effects=True, vmem_limit_bytes=44 << 20),
    )(
        *(
            pltpu.with_memory_space_constraint(value, pltpu.HBM)
            for value in (
                encoded_anchor,
                encoded_target,
                matched_target.reshape(4, 128),
                anchor_logzeta.reshape(4, 128),
                target_logzeta_saved.reshape(1, rows),
                heat_values,
            )
        ),
        matchup_position,
    )
    return pl.pallas_call(
        finish_kernel,
        out_shape=(jax.ShapeDtypeStruct((rows, width), F32), jax.ShapeDtypeStruct((rows, width), F32)),
        in_specs=[vmem] * 9,
        out_specs=[anywhere] * 2,
        scratch_shapes=[pltpu.VMEM((2, rows, width), F32), dma((4,))],
        compiler_params=pltpu.CompilerParams(vmem_limit_bytes=32 << 20),
    )(*pieces)


def solution(mesh):
    both = ("grp", "blk")
    return jax.shard_map(
        on_device,
        mesh=mesh,
        in_specs=(P(both, None), P(both, None), P(both), P(both), P(both), P("grp"), P("grp")),
        out_specs=(P(both, None), P(both, None)),
        check_vma=False,
    )
```

```python
import functools
import math

import jax
import jax.numpy as jnp
from jax import lax
from jax.experimental import pallas as pl
from jax.experimental.pallas import tpu as pltpu
from jax.sharding import PartitionSpec as P

MESH = pl.DeviceIdType.MESH
BF, F32 = jnp.bfloat16, jnp.float32
NT = (((1,), (1,)), ((), ()))
TN = (((0,), (0,)), ((), ()))


def unit_rows(block):
    floats = block.astype(F32)
    inverse = lax.rsqrt(jnp.sum(floats * floats, axis=1, keepdims=True) + 1e-06)
    return inverse, floats * inverse


def exchange_kernel(
    a_hbm, b_hbm, match_hbm, la_hbm, lb_hbm, heat_hbm, which,
    scale_out, a_own, b_own, da_own, da_left, da_right, db_own, db_core, db_far,
    a_in, b_in, ua, ub, match, la, lb, eb, ids, ea_col, match_col, da, db, da_out, opp_in, db_out, db_other, core_in, heat,
    in_sem, send_sems, recv_sems,
):
    rows = a_hbm.shape[0]
    half, quarter = rows // 2, rows // 4
    first, second = pl.ds(0, half), pl.ds(half, half)
    grp, blk = lax.axis_index("grp"), lax.axis_index("blk")
    x, y, core = blk // 4, (blk // 2) % 2, blk % 2

    def at(px, py, pc):
        return px * 4 + py * 2 + pc

    left, right = at((x + 3) % 4, y, core), at((x + 1) % 4, y, core)
    other, far, far_other = at(x, y, 1 - core), at(x, 1 - y, core), at(x, 1 - y, 1 - core)

    barrier = pltpu.get_barrier_semaphore()
    for peer in (left, right, other, far):
        pl.semaphore_signal(barrier, inc=1, device_id=(grp, peer), device_id_type=MESH)

    loads = [
        pltpu.make_async_copy(src, dst, in_sem.at[k])
        for k, (src, dst) in enumerate(
            ((a_hbm, a_own), (b_hbm, b_own), (match_hbm, match.at[0]), (la_hbm, la.at[0]), (lb_hbm, lb.at[0]),
             (heat_hbm, heat))
        )
    ]
    for load in loads:
        load.start()

    copies = []

    def send(src, dst, peer):
        k = len(copies)
        copy = pltpu.make_async_remote_copy(
            src_ref=src, dst_ref=dst, send_sem=send_sems.at[k], recv_sem=recv_sems.at[k],
            device_id=(grp, peer), device_id_type=MESH,
        )
        copy.start()
        copies.append(copy)
        return copy

    def take_a(group, pieces):
        ua[group] = unit_rows(a_own[...] if group == 0 else a_in[group - 1])[1].astype(BF)
        columns = {}
        for source in sorted({source for source, _ in pieces}):
            columns[source] = (jnp.exp(-la[source]).T, match[source].astype(F32).T)
        for k, (source, quarter) in enumerate(pieces):
            into = pl.ds(k * 128, 128)
            weights, partners = columns[source]
            ea_col[group, into, :] = jnp.broadcast_to(weights[:, quarter : quarter + 1], (128, 128))
            match_col[group, into, :] = jnp.broadcast_to(partners[:, quarter : quarter + 1], (128, 128))

    def take_b(j, part):
        into = pl.ds(part * half, half)
        ub[j, into] = unit_rows((b_own if j == 0 else b_in.at[j - 1])[into])[1].astype(BF)
        if j < 2:
            source, owner, begin = j, (blk, other)[j], part * half
        else:
            source, owner, begin = 2 + part, (far, far_other)[part], (j - 2) * half
        eb[j, :, part * half : part * half + half] = jnp.exp(-lb[source, :, begin : begin + half])
        along = lax.broadcasted_iota(jnp.int32, (1, half), 1)
        ids[j, :, part * half : part * half + half] = (along + (owner * rows + begin)).astype(F32)

    begun = set()

    def add(into, term, key):
        if key in begun:
            into[...] += term
        else:
            into[...] = term
        begun.add(key)

    def raw_scores(group, j, part):
        return lax.dot_general(ua[group], ub[j, pl.ds(part * half, half)], NT, preferred_element_type=F32)

    def spend(raw, group, j, part):
        here = pl.ds(part * half, half)
        along = slice(part * half, part * half + half)
        chance = jnp.exp2(raw * scale)
        reps = half // 128
        weight = jnp.concatenate([ea_col[group]] * reps, axis=1) + eb[j, :, along]
        paired = jnp.concatenate([match_col[group]] * reps, axis=1) == ids[j, :, along]
        value = chance * weight
        coupling = jnp.where(paired, value - 2.0, value).astype(BF)
        rows_term = jnp.dot(coupling, ub[j, here], preferred_element_type=F32)
        add(da_own if group == 0 else da.at[group - 1], rows_term, ("a", group))
        columns_term = lax.dot_general(coupling, ua[group], TN, preferred_element_type=F32)
        add((db_own if j == 0 else db.at[j - 1]).at[here], columns_term, ("b", j, part))

    def pairs(*todo):
        units = []
        for group, j, *part in todo:
            units += [(group, j, p) for p in (part or (0, 1))]
        ahead = raw_scores(*units[0])
        for k, unit in enumerate(units):
            raw = ahead
            if k + 1 < len(units):
                ahead = raw_scores(*units[k + 1])
            spend(raw, *unit)

    pl.semaphore_wait(barrier, 4)
    quarters = [pl.ds(k * quarter, quarter) for k in range(4)]
    small_left = [send(match_hbm, match.at[2], left), send(la_hbm, la.at[2], left)]
    small_right = [send(match_hbm, match.at[1], right), send(la_hbm, la.at[1], right)]
    lb_other = send(lb_hbm, lb.at[1], other)
    lb_far = send(lb_hbm, lb.at[2], far)
    early_right = [send(a_hbm.at[quarters[k]], a_in.at[0, quarters[k]], right) for k in (0, 1)]
    early_left = [send(a_hbm.at[quarters[k]], a_in.at[0, quarters[k]], left) for k in (2, 3)]
    b_other = send(b_hbm, b_in.at[0], other)
    far_a = send(b_hbm.at[first], b_in.at[1, first], far)
    far_b = send(b_hbm.at[second], b_in.at[2, first], far)

    for load in loads:
        load.wait()
    temperature = jnp.float32(0.0)
    for k in range(heat.shape[0]):
        temperature += jnp.where(which[0] == k, heat[k], 0.0)
    scale = math.log2(math.e) / jnp.broadcast_to(temperature, (1, 1))
    scale_out[...] = jnp.broadcast_to(1.0 / jnp.broadcast_to(temperature, (1, 1)), (8, 128))
    take_a(0, [(0, 0), (0, 1), (0, 2), (0, 3)])
    take_b(0, 0)
    take_b(0, 1)
    pairs((0, 0))
    b_other.wait_recv()
    lb_other.wait_recv()
    take_b(1, 0)
    take_b(1, 1)
    pairs((0, 1))

    opp = []
    for k in (0, 1):
        early_right[k].wait_recv()
        opp.append(send(a_in.at[0, quarters[k]], a_in.at[1, quarters[k]], right))
        early_left[k].wait_recv()
        opp.append(send(a_in.at[0, quarters[k + 2]], a_in.at[1, quarters[k + 2]], left))
    for copy in small_left + small_right:
        copy.wait_recv()
    small_on = [send(match.at[1], match.at[3], right), send(la.at[1], la.at[3], right)]
    lb_far.wait_recv()
    lb_on = send(lb.at[2], lb.at[3], other)

    take_a(1, [(1, 0), (1, 1), (2, 2), (2, 3)])
    pairs((1, 0), (1, 1))

    late_left = send(a_hbm.at[first], a_in.at[2, second], left)
    late_right = send(a_hbm.at[second], a_in.at[2, first], right)
    far_a.wait_recv()
    far_a_on = send(b_in.at[1, first], b_in.at[1, second], other)
    take_b(2, 0)
    pairs((1, 2, 0), (0, 2, 0))

    far_b.wait_recv()
    far_b_on = send(b_in.at[2, first], b_in.at[2, second], other)
    lb_on.wait_recv()
    far_a_on.wait_recv()
    take_b(2, 1)
    take_b(3, 0)
    pairs((1, 2, 1), (0, 2, 1))

    for copy in small_on + opp:
        copy.wait_recv()
    take_a(2, [(3, 0), (3, 1), (3, 2), (3, 3)])
    pairs((2, 0), (2, 1), (2, 2), (2, 3, 0))

    far_b_on.wait_recv()
    take_b(3, 1)
    pairs((2, 3, 1))
    da_out[1] = da[1].astype(BF)
    part_right = send(da_out.at[1, first], opp_in.at[first], right)
    part_left = send(da_out.at[1, second], opp_in.at[second], left)
    late_left.wait_recv()
    late_right.wait_recv()
    take_a(3, [(1, 2), (1, 3), (2, 0), (2, 1)])
    pairs((3, 2, 1), (3, 2, 0))
    db_out[0] = db[1, half:rows].astype(BF)
    core_a = send(db_out.at[0], core_in.at[0], other)

    pairs((1, 3), (0, 3))
    da_out[0] = da[0].astype(BF)
    sum_left = send(da_out.at[0, first], da_right.at[first], left)
    sum_right = send(da_out.at[0, second], da_left.at[second], right)
    core_a.wait_recv()
    db_out[2] = (db[1, 0:half] + core_in[0].astype(F32)).astype(BF)
    sum_far_a = send(db_out.at[2], db_far.at[first], far)

    pairs((3, 3, 1), (3, 3, 0))
    db_out[1] = db[2, half:rows].astype(BF)
    core_b = send(db_out.at[1], core_in.at[1], other)

    pairs((3, 1), (3, 0))
    core_b.wait_recv()
    db_out[3] = (db[2, 0:half] + core_in[1].astype(F32)).astype(BF)
    sum_far_b = send(db_out.at[3], db_far.at[second], far)
    db_other[...] = db[0].astype(BF)
    sum_other = send(db_other, db_core, other)

    part_right.wait_recv()
    part_left.wait_recv()
    da_out[2, 0:half, :] = (da[2, 0:half, :] + opp_in[half:rows, :].astype(F32)).astype(BF)
    da_out[2, half:rows, :] = (da[2, half:rows, :] + opp_in[0:half, :].astype(F32)).astype(BF)
    last_left = send(da_out.at[2, first], da_right.at[second], left)
    last_right = send(da_out.at[2, second], da_left.at[first], right)

    for copy in (sum_left, sum_right, sum_other, sum_far_a, last_left, last_right, sum_far_b):
        copy.wait_recv()
    for copy in copies:
        copy.wait_send()


def finish_kernel(
    scale, a, b, da_own, da_left, da_right, db_own, db_core, db_far, out_a, out_b, result, sems
):
    rows = a.shape[0]
    quarter = rows // 4
    by_temperature = scale[0:1, 0:1]

    def tangent(block, total):
        inverse, unit = unit_rows(block)
        dunit = total * by_temperature
        return inverse * (dunit - unit * jnp.sum(unit * dunit, axis=1, keepdims=True))

    copies = []
    for which, (block, total, parts, out) in enumerate(
        ((b, db_own, (db_core, db_far), out_b), (a, da_own, (da_left, da_right), out_a))
    ):
        for k in range(4):
            part = pl.ds(k * quarter, quarter)
            summed = total[part] + parts[0][part].astype(F32) + parts[1][part].astype(F32)
            result[which, part] = tangent(block[part], summed)
            copies.append(pltpu.make_async_copy(result.at[which, part], out.at[part], sems.at[4 * which + k]))
            copies[-1].start()
    for copy in copies:
        copy.wait()


def on_device(encoded_anchor, encoded_target, matched_target, anchor_logzeta, target_logzeta_saved, heat_values, matchup_position):
    rows, width = encoded_anchor.shape
    anywhere = pl.BlockSpec(memory_space=pl.ANY)
    vmem = pl.BlockSpec(memory_space=pltpu.VMEM)
    dma = pltpu.SemaphoreType.DMA
    block = jax.ShapeDtypeStruct((rows, width), BF)
    pieces = pl.pallas_call(
        exchange_kernel,
        out_shape=(
            jax.ShapeDtypeStruct((8, 128), F32),
            block,
            block,
            jax.ShapeDtypeStruct((rows, width), F32),
            block,
            block,
            jax.ShapeDtypeStruct((rows, width), F32),
            block,
            block,
        ),
        in_specs=[anywhere] * 6 + [pl.BlockSpec(memory_space=pltpu.SMEM)],
        out_specs=[vmem] * 9,
        scratch_shapes=[
            pltpu.VMEM((3, rows, width), BF),
            pltpu.VMEM((3, rows, width), BF),
            pltpu.VMEM((4, rows, width), BF),
            pltpu.VMEM((4, rows, width), BF),
            pltpu.VMEM((4, 4, 128), jnp.int32),
            pltpu.VMEM((4, 4, 128), F32),
            pltpu.VMEM((4, 1, rows), F32),
            pltpu.VMEM((4, 1, rows), F32),
            pltpu.VMEM((4, 1, rows), F32),
            pltpu.VMEM((4, rows, 128), F32),
            pltpu.VMEM((4, rows, 128), F32),
            pltpu.VMEM((3, rows, width), F32),
            pltpu.VMEM((3, rows, width), F32),
            pltpu.VMEM((3, rows, width), BF),
            pltpu.VMEM((rows, width), BF),
            pltpu.VMEM((4, rows // 2, width), BF),
            pltpu.VMEM((rows, width), BF),
            pltpu.VMEM((2, rows // 2, width), BF),
            pltpu.SMEM((4,), F32),
            dma((6,)),
            dma((36,)),
            dma((36,)),
        ],
        compiler_params=pltpu.CompilerParams(collective_id=7, has_side_effects=True, vmem_limit_bytes=44 << 20),
    )(
        *(
            pltpu.with_memory_space_constraint(value, pltpu.HBM)
            for value in (
                encoded_anchor,
                encoded_target,
                matched_target.reshape(4, 128),
                anchor_logzeta.reshape(4, 128),
                target_logzeta_saved.reshape(1, rows),
                heat_values,
            )
        ),
        matchup_position,
    )
    return pl.pallas_call(
        finish_kernel,
        out_shape=(jax.ShapeDtypeStruct((rows, width), F32), jax.ShapeDtypeStruct((rows, width), F32)),
        in_specs=[vmem] * 9,
        out_specs=[anywhere] * 2,
        scratch_shapes=[pltpu.VMEM((2, rows, width), F32), dma((8,))],
        compiler_params=pltpu.CompilerParams(vmem_limit_bytes=32 << 20),
    )(*pieces)


def solution(mesh):
    both = ("grp", "blk")
    return jax.shard_map(
        on_device,
        mesh=mesh,
        in_specs=(P(both, None), P(both, None), P(both), P(both), P(both), P("grp"), P("grp")),
        out_specs=(P(both, None), P(both, None)),
        check_vma=False,
    )
```
